32 devices in a mesh: seq: 8 (over y, x, core), wt: 4 (over z).
Axes of the slice: x: 2, y: 2, z: 4, core: 2. Of those that a mesh axis runs over, the one named last changes fastest.
Arguments:
- block_input: bfloat16 [10240, 1024], P(('seq', 'wt')), may hold values from -6 to 6
- positions: int32 [10240], P(('seq', 'wt')), may hold values from 0 to 9919, as said below
- norm_gain_attn: bfloat16 [1024], P(('seq', 'wt')), may hold values from 0.5 to 1.5
- w_qkv: bfloat16 [1024, 3072], P(('seq', 'wt')), may hold values from -0.1875 to 0.1875
- w_out: bfloat16 [1024, 1024], P(('seq', 'wt')), may hold values from -0.5 to 0.5
- norm_gain_mlp: bfloat16 [1024], P(('seq', 'wt')), may hold values from 0.5 to 1.5
- w_in: bfloat16 [1024, 5248], P(('seq', 'wt')), may hold values from -0.1875 to 0.1875
- w_down: bfloat16 [1024, 2624], P(('seq', 'wt')), may hold values from -0.125 to 0.125
- cotangent: bfloat16 [10240, 1024], P(('seq', 'wt')), may hold values from -6 to 6
Outputs:
- block_output: bfloat16 [10240, 1024], P(('seq', 'wt'))
- input_grad: bfloat16 [10240, 1024], P(('seq', 'wt'))
- grad_gain_attn: float32 [1024], P(('seq', 'wt'))
- grad_qkv: float32 [1024, 3072], P(('seq', 'wt'))
- grad_out: float32 [1024, 1024], P(('seq', 'wt'))
- grad_gain_mlp: float32 [1024], P(('seq', 'wt'))
- grad_in: float32 [1024, 5248], P(('seq', 'wt'))
- grad_down: float32 [1024, 2624], P(('seq', 'wt'))
The draws below stay inside these ranges and needn't reach their ends.
Inputs may be any that keep to these rules, and one draw needn't show every extreme that they name: positions count up by one from 0 within each document, and a document begins at token 0; one long document begins inside the first aligned block of 320 tokens at an offset of 64 to 256 and ends at the same offset inside the last aligned block, so that it holds 9920 tokens; the tokens before it and after it form further documents of varying lengths.
All inputs are finite; a program needn't handle non-finite values.
Results may differ from the reference program's by a relative error of at most 0.015.
Values may be sent and summed in bfloat16 or wider, within the bound.
A program may use at most 256 MiB of HBM per device.

```python
import jax
import jax.numpy as jnp
from jax import lax

D = 1024
HEADS = 16
HEAD_DIM = 64
FF = 2624
WING = 64
TOK_DEV = 320
TOKENS = 10240


def draw_positions(key, part):
    key = jax.random.fold_in(key, 7)
    offset_key, break_key = jax.random.split(key)
    offset = jax.random.randint(offset_key, (), WING, TOK_DEV - WING + 1)
    token_index = jnp.arange(TOKENS, dtype=jnp.int32)
    second_start = offset
    third_start = TOKENS - TOK_DEV + offset
    breaks = jax.random.randint(break_key, (TOKENS,), 0, 8) == 0
    outside = (token_index < second_start) | (token_index > third_start)
    is_start = (token_index == 0) | (token_index == second_start) | (token_index == third_start)
    is_start = is_start | breaks & outside
    marked = jnp.where(is_start, token_index, 0).astype(jnp.int32)
    latest = lax.cummax(marked, axis=0)
    return (token_index - latest).astype(jnp.int32)


def strengthened(entries, key, source, target, blocks, factor):
    def block_of(axis_at):
        return (jnp.arange(entries.shape[axis_at]) // (entries.shape[axis_at] // blocks)).reshape((-1,) + (1,) * (entries.ndim - 1 - axis_at))

    first = jax.random.permutation(key, blocks)[block_of(target)]
    far = (block_of(target) + blocks // 2) % blocks
    return jnp.where((block_of(source) == first) | (block_of(source) == far), factor * entries, entries)


def level_of(rng, extent, cuts, smallest, high):
    def one(position, shards_of):
        steps = jax.random.uniform(jax.random.fold_in(jax.random.fold_in(rng, 6), position), (shards_of,), jnp.float32, smallest / len(cuts), high / len(cuts))
        return jnp.repeat(jnp.exp(steps), extent[position] // shards_of).reshape((-1,) + (1,) * (len(extent) - position - 1))

    level = one(*cuts[0])
    for cut in cuts[1:]:
        level = level * one(*cut)
    return level


def gaussian(stream_key, shape, scale, bound, cuts=(), held_as=jnp.bfloat16):
    result = scale * jax.random.normal(stream_key, shape, jnp.float32)
    if cuts:
        result = result * level_of(stream_key, shape, cuts, -0.22, 0.18)
    return jnp.clip(result, -bound, bound).astype(held_as)


def noise_with(stream_key, dims, deviation, reach, cuts, heavy, kind=jnp.bfloat16):
    entries = deviation * jax.random.normal(stream_key, dims, jnp.float32)
    if cuts:
        entries = entries * level_of(stream_key, dims, cuts, -0.22, 0.18)
    return jnp.clip(strengthened(entries, jax.random.fold_in(stream_key, 3), *heavy), -reach, reach).astype(kind)


def setup_inputs(seed: int = 0) -> dict:
    splits = jax.random.split(jax.random.key(seed), 10)
    block_input = gaussian(splits[0], (TOKENS, D), 1.0, 6.0, ((0, 32),))
    positions = draw_positions(jax.random.fold_in(splits[9], 71), 0)
    norm_gain_attn = jnp.clip(1.0 + 0.1 * jax.random.normal(splits[2], (D,), jnp.float32), 0.5, 1.5).astype(jnp.bfloat16)
    w_qkv = gaussian(splits[3], (D, 3 * D), D ** -0.5, 0.1875, ((0, 32),))
    w_out = gaussian(splits[4], (D, D), (D // 8) ** -0.5, 0.5, ((0, 32),))
    norm_gain_mlp = jnp.clip(1.0 + 0.1 * jax.random.normal(splits[5], (D,), jnp.float32), 0.5, 1.5).astype(jnp.bfloat16)
    w_in = gaussian(splits[6], (D, 2 * FF), D ** -0.5, 0.1875, ((0, 32),))
    w_down = gaussian(splits[7], (D, FF), FF ** -0.5, 0.125, ((0, 32),))
    cotangent = noise_with(splits[8], (TOKENS, D), 1.0, 6.0, ((0, 32),), (0, 1, 32, 2.75))
    return {"block_input": block_input, "positions": positions, "norm_gain_attn": norm_gain_attn, "w_qkv": w_qkv, "w_out": w_out, "norm_gain_mlp": norm_gain_mlp, "w_in": w_in, "w_down": w_down, "cotangent": cotangent}


@jax.custom_vjp
def low(v):
    return lax.optimization_barrier(v.astype(jnp.bfloat16)).astype(jnp.float32)

@jax.custom_vjp
def low_back(v):
    return v

def low_keep(v):
    return (low(v), None)

def low_pass(kept, grad):
    return (grad,)

def back_keep(v):
    return (v, None)

def back_low(kept, grad):
    return (low(grad),)
low.defvjp(low_keep, low_pass)
low_back.defvjp(back_keep, back_low)
PRECISE = lax.Precision.HIGHEST
EPSILON = 1e-05

def layer_norm(rows, gain):
    centered = rows - lax.optimization_barrier(jnp.mean(rows, axis=-1, keepdims=True))
    spread = lax.optimization_barrier(jnp.mean(centered * centered, axis=-1, keepdims=True))
    return centered * lax.rsqrt(spread + EPSILON) * gain

def rotate_half(vectors):
    middle = vectors.shape[-1] // 2
    return jnp.concatenate([-vectors[..., middle:], vectors[..., :middle]], axis=-1)

def angles(positions, head_width):
    middle = head_width // 2
    freqs = 10000.0 ** (-2.0 * jnp.arange(middle, dtype=jnp.float32) / head_width)
    phase = positions.astype(jnp.float32)[:, None] * freqs[None, :]
    phase = jnp.concatenate([phase, phase], axis=-1)[:, None, :]
    return (jnp.cos(phase), jnp.sin(phase))

def rotary(vectors, cosine, sine):
    return vectors * cosine + rotate_half(vectors) * sine

def attend(query_rot, key_rot, values, positions):
    token_total = query_rot.shape[0]
    block_rows = min(512, token_total)
    key_count = block_rows + 2 * WING
    edge_pad = ((WING, WING), (0, 0), (0, 0))
    key_ext = jnp.pad(key_rot, edge_pad)
    value_ext = jnp.pad(values, edge_pad)
    padded = jnp.pad(positions, (WING, WING))
    scaling = HEAD_DIM ** (-0.5)

    def attend_block(block_start):
        query_block = lax.dynamic_slice_in_dim(query_rot, block_start, block_rows, 0)
        key_block = lax.dynamic_slice_in_dim(key_ext, block_start, key_count, 0)
        value_block = lax.dynamic_slice_in_dim(value_ext, block_start, key_count, 0)
        query_pos = lax.dynamic_slice_in_dim(positions, block_start, block_rows, 0)
        key_pos = lax.dynamic_slice_in_dim(padded, block_start, key_count, 0)
        query_index = block_start + jnp.arange(block_rows, dtype=jnp.int32)
        key_index = block_start - WING + jnp.arange(key_count, dtype=jnp.int32)
        offset = query_index[:, None] - key_index[None, :]
        allowed = (jnp.abs(offset) <= WING) & (key_index[None, :] >= 0) & (key_index[None, :] < token_total)
        allowed = allowed & (query_pos[:, None] - key_pos[None, :] == offset)
        scores = low_back(jnp.einsum('qhd,khd->hqk', query_block, key_block, precision=PRECISE) * scaling)
        scores = jnp.where(allowed[None], scores, -1e+30)
        largest = lax.optimization_barrier(jnp.max(scores, axis=-1, keepdims=True))
        weights = jnp.exp(scores - largest)
        probs = low(weights / lax.optimization_barrier(jnp.sum(weights, axis=-1, keepdims=True)))
        return jnp.einsum('hqk,khd->qhd', probs, value_block, precision=PRECISE)
    starts = jnp.arange(token_total // block_rows, dtype=jnp.int32) * block_rows
    mixed = lax.map(jax.checkpoint(attend_block), starts)
    return mixed.reshape(token_total, -1)

def reference(block_input, positions, norm_gain_attn, w_qkv, w_out, norm_gain_mlp, w_in, w_down, cotangent):
    cosine, sine = angles(positions, HEAD_DIM)

    def forward(inputs, gain_attn, weight_qkv, weight_out, gain_mlp, weight_in, weight_down):
        token_total = inputs.shape[0]
        act_one = low(layer_norm(inputs, gain_attn))
        qkv = low_back(jnp.dot(act_one, weight_qkv, precision=PRECISE))
        query = qkv[:, :D].reshape(token_total, HEADS, HEAD_DIM)
        keys = qkv[:, D:2 * D].reshape(token_total, HEADS, HEAD_DIM)
        values = qkv[:, 2 * D:].reshape(token_total, HEADS, HEAD_DIM)
        query_rot = low(rotary(query, cosine, sine))
        key_rot = low(rotary(keys, cosine, sine))
        attn = low(low_back(attend(query_rot, key_rot, low(values), positions)))
        resid = inputs + low_back(jnp.dot(attn, weight_out, precision=PRECISE))
        act_two = low(layer_norm(resid, gain_mlp))
        upward = low_back(jnp.dot(act_two, weight_in, precision=PRECISE))
        hidden = low(jax.nn.gelu(upward[:, :FF], approximate=False) * upward[:, FF:])
        return resid + low_back(jnp.dot(hidden, weight_down.T, precision=PRECISE))
    output, pullback = jax.vjp(forward, block_input.astype(jnp.float32), norm_gain_attn.astype(jnp.float32), w_qkv.astype(jnp.float32), w_out.astype(jnp.float32), norm_gain_mlp.astype(jnp.float32), w_in.astype(jnp.float32), w_down.astype(jnp.float32))
    grads = pullback(cotangent.astype(jnp.float32))
    return (output.astype(jnp.bfloat16), grads[0].astype(jnp.bfloat16), grads[1], grads[2], grads[3], grads[4], grads[5], grads[6])
```

```python
import jax
import jax.numpy as jnp
from jax import lax
from jax.sharding import PartitionSpec as P

HEADS = 16
HEAD_DIM = 64
WING = 64


EPSILON = 1e-05


def padded_2(block, sides, width):
    for axis, dim in sides:
        count = lax.axis_size(axis)
        forward = [(i, i + 1) for i in range(count - 1)]
        backward = [(target, source) for source, target in forward]
        low = lax.ppermute(
            lax.slice_in_dim(block, block.shape[dim] - width, None, axis=dim), axis, forward
        )
        high = lax.ppermute(lax.slice_in_dim(block, 0, width, axis=dim), axis, backward)
        block = jnp.concatenate([low, block, high], axis=dim)
    return block


def shifted(block, axis, distance):
    devices = range(lax.axis_size(axis))
    route = [(i - distance, i) for i in devices if i - distance in devices]
    return lax.ppermute(block, axis, route)


def layer_norm(rows, gain):
    centered = rows - jnp.mean(rows, axis=-1, keepdims=True)
    spread = jnp.mean(centered * centered, axis=-1, keepdims=True)
    return centered * lax.rsqrt(spread + EPSILON) * gain


def rotate_half(vectors):
    middle = vectors.shape[-1] // 2
    return jnp.concatenate([-vectors[..., middle:], vectors[..., :middle]], axis=-1)


def angles(positions, head_width):
    middle = head_width // 2
    freqs = 10000.0 ** (-2.0 * jnp.arange(middle, dtype=jnp.float32) / head_width)
    phase = positions.astype(jnp.float32)[:, None] * freqs[None, :]
    phase = jnp.concatenate([phase, phase], axis=-1)[:, None, :]
    return (jnp.cos(phase), jnp.sin(phase))


def rotary(vectors, cosine, sine):
    return vectors * cosine + rotate_half(vectors) * sine


def rotary_back(grads, cosine, sine):
    return grads * cosine - rotate_half(grads * sine)


def gated(first, second):
    return jax.nn.gelu(first, approximate=False) * second


def device_count():
    return lax.axis_size(("seq", "wt"))


def swapped(block, mask):
    route = [(i, i ^ mask) for i in range(device_count())]
    return lax.ppermute(block, ("seq", "wt"), route)


def stage_bits(flip):
    near = lax.axis_size("wt")
    far = []
    bit = near
    while bit < device_count():
        far.append(bit)
        bit *= 2
    first, rest = far[0], far[1:]
    return near, first, rest[::-1] if flip else rest


def gather_rel(block, flip):
    near, first, rest = stage_bits(flip)
    levels = len(rest) + 1
    held = jnp.concatenate([block] + [swapped(block, j) for j in range(1, near)], axis=0)
    held = held.reshape((1,) * levels + held.shape)
    for bit in rest + [first]:
        axis = levels - 1 - ((bit // near).bit_length() - 1)
        held = jnp.concatenate([held, swapped(held, bit)], axis=axis)
    return held.reshape(-1, block.shape[1])


def scatter_rel(left, right, flip):
    near, first, rest = stage_bits(flip)
    rows = left.shape[1] // device_count()
    levels = len(rest) + 1
    tokens = left.shape[0]
    parts = left.reshape((tokens,) + (2,) * levels + (near * rows,))
    first_axis = levels
    second_axis = levels - ((rest[0] // near).bit_length() - 1)

    def part(core, second):
        piece = lax.slice_in_dim(parts, core, core + 1, axis=first_axis)
        piece = lax.slice_in_dim(piece, second, second + 1, axis=second_axis)
        return piece.reshape(tokens, -1)

    def product(core, second):
        return lax.dot_general(
            part(core, second),
            right,
            (((0,), (0,)), ((), ())),
            preferred_element_type=jnp.float32,
        )

    got_far = swapped(product(1, 1).astype(jnp.bfloat16), first)
    got_near = swapped(product(1, 0).astype(jnp.bfloat16), first)
    far = (product(0, 1) + got_far.astype(jnp.float32)).astype(jnp.bfloat16)
    got = swapped(far, rest[0])
    total = product(0, 0) + got_near.astype(jnp.float32) + got.astype(jnp.float32)
    remaining = sorted(rest[1:], reverse=True)
    total = total.reshape((2,) * len(remaining) + (near, rows, right.shape[1]))
    for bit in rest[1:]:
        axis = remaining.index(bit)
        keep = lax.slice_in_dim(total, 0, 1, axis=axis)
        send = lax.slice_in_dim(total, 1, 2, axis=axis).astype(jnp.bfloat16)
        total = keep + swapped(send, bit).astype(jnp.float32)
    total = total.reshape(near, rows, right.shape[1])
    result = total[0]
    for j in range(1, near):
        result = result + swapped(total[j].astype(jnp.bfloat16), j).astype(jnp.float32)
    return result


def scatter_gains(gains):
    total = gains.reshape(gains.shape[0], device_count(), -1).swapaxes(0, 1)
    while total.shape[0] > 1:
        half = total.shape[0] // 2
        total = total[:half] + swapped(total[half:], half)
    return total[0]


def block_mask(positions, block_start, block_rows, token_total, at_first, at_last):
    key_count = block_rows + 2 * WING
    query_index = block_start + jnp.arange(block_rows, dtype=jnp.int32)
    key_index = block_start - WING + jnp.arange(key_count, dtype=jnp.int32)
    padded = jnp.pad(positions, (WING, WING))
    offset = query_index[:, None] - key_index[None, :]
    inside = (key_index >= 0) & (key_index < token_total)
    same_doc = jnp.where(inside[None, :], positions[:, None] - padded[None, :] == offset, True)
    present = ((key_index >= 0) | jnp.logical_not(at_first)) & (
        (key_index < token_total) | jnp.logical_not(at_last)
    )
    return (jnp.abs(offset) <= WING) & same_doc & present[None, :]


def block_probs(query_block, key_block, allowed):
    scaling = HEAD_DIM ** (-0.5)
    scores = (
        jnp.einsum("qhd,khd->hqk", query_block, key_block, preferred_element_type=jnp.float32)
        * scaling
    )
    scores = jnp.where(allowed[None], scores, -1e30)
    largest = jnp.max(scores, axis=-1, keepdims=True)
    weights = jnp.exp(scores - largest)
    return weights / jnp.sum(weights, axis=-1, keepdims=True)


def on_device(
    block_input, positions, norm_gain_attn, w_qkv, w_out, norm_gain_mlp, w_in, w_down, cotangent
):
    token_total = block_input.shape[0]
    width = block_input.shape[1]
    scaling = HEAD_DIM ** (-0.5)
    device_index = lax.axis_index(("seq", "wt"))
    hidden_units = w_down.shape[1]
    cut = w_qkv.shape[1] // 2
    gains = jnp.stack([norm_gain_attn, norm_gain_mlp], axis=1)
    gains = jnp.pad(gains, ((0, 0), (0, 126)))
    full_one = gather_rel(jnp.concatenate([w_qkv[:, :cut], gains], axis=1), False)
    full_two = gather_rel(w_qkv[:, cut:], True)
    full_out = gather_rel(w_out, False)
    full_first = gather_rel(w_in[:, :hidden_units], False)
    full_second = gather_rel(w_in[:, hidden_units:], True)
    full_down = gather_rel(w_down, True)
    gain_attn = full_one[:, cut]
    gain_mlp = full_one[:, cut + 1]
    full_one = full_one[:, :cut]
    order = jnp.arange(width, dtype=jnp.int32) ^ (device_index * w_out.shape[0])
    swap = (order[:, None] == jnp.arange(width, dtype=jnp.int32)[None, :]).astype(jnp.bfloat16)

    def reorder(rows):
        return jnp.dot(rows, swap, preferred_element_type=jnp.float32).astype(jnp.bfloat16)

    full_out = reorder(full_out)
    block_input = reorder(block_input)
    cotangent = reorder(cotangent)
    at_first = device_index == 0
    at_last = device_index == lax.axis_size(("seq", "wt")) - 1
    inputs = block_input.astype(jnp.float32)
    normed_one, norm_one_back = jax.vjp(layer_norm, inputs, gain_attn.astype(jnp.float32))
    act_one = normed_one.astype(jnp.bfloat16)
    qkv = jnp.concatenate(
        [
            jnp.dot(act_one, full_one, preferred_element_type=jnp.float32),
            jnp.dot(act_one, full_two, preferred_element_type=jnp.float32),
        ],
        axis=1,
    )
    cosine, sine = angles(positions, HEAD_DIM)
    query_rot = rotary(qkv[:, :width].reshape(token_total, HEADS, HEAD_DIM), cosine, sine).astype(
        jnp.bfloat16
    )
    key_rot = rotary(
        qkv[:, width : 2 * width].reshape(token_total, HEADS, HEAD_DIM), cosine, sine
    ).astype(jnp.bfloat16)
    value_low = qkv[:, 2 * width :].astype(jnp.bfloat16)
    paired = jnp.concatenate([key_rot.reshape(token_total, width), value_low], axis=1)
    edged = padded_2(paired, ((("seq", "wt"), 0),), WING)
    key_ext = edged[:, :width].reshape(-1, HEADS, HEAD_DIM)
    value_ext = edged[:, width:].reshape(-1, HEADS, HEAD_DIM)
    block_rows = min(512, token_total)
    starts = jnp.arange(token_total // block_rows, dtype=jnp.int32) * block_rows

    def slices(block_start):
        allowed = block_mask(positions, block_start, block_rows, token_total, at_first, at_last)
        return (query_rot, key_ext, value_ext, allowed)

    def forward_block(block_start):
        query_block, key_block, value_block, allowed = slices(block_start)
        probs = block_probs(query_block, key_block, allowed)
        mixed = jnp.einsum(
            "hqk,khd->qhd",
            probs.astype(jnp.bfloat16),
            value_block,
            preferred_element_type=jnp.float32,
        )
        return (mixed, probs)

    mixed, stored = lax.map(forward_block, starts)
    attn = reorder(mixed.reshape(token_total, width).astype(jnp.bfloat16))
    resid = inputs + jnp.dot(attn, full_out, preferred_element_type=jnp.float32)
    normed_two, norm_two_back = jax.vjp(layer_norm, resid, gain_mlp.astype(jnp.float32))
    act_two = normed_two.astype(jnp.bfloat16)
    first = jnp.dot(act_two, full_first, preferred_element_type=jnp.float32)
    second = jnp.dot(act_two, full_second, preferred_element_type=jnp.float32)
    gated_value, gated_back = jax.vjp(gated, first, second)
    hidden = gated_value.astype(jnp.bfloat16)
    output = resid + jnp.einsum("tf,df->td", hidden, full_down, preferred_element_type=jnp.float32)
    block_output = reorder(output.astype(jnp.bfloat16))
    grad_down = scatter_rel(cotangent, hidden, True)
    dhidden = jnp.dot(cotangent, full_down, preferred_element_type=jnp.float32)
    dfirst, dsecond = gated_back(dhidden)
    dfirst = dfirst.astype(jnp.bfloat16)
    dsecond = dsecond.astype(jnp.bfloat16)
    grad_in = jnp.concatenate(
        [scatter_rel(act_two, dfirst, False), scatter_rel(act_two, dsecond, True)], axis=1
    )
    dact_two = jnp.einsum(
        "tf,df->td", dfirst, full_first, preferred_element_type=jnp.float32
    ) + jnp.einsum("tf,df->td", dsecond, full_second, preferred_element_type=jnp.float32)
    dresid_norm, grad_gain_mlp = norm_two_back(dact_two)
    dresid = cotangent.astype(jnp.float32) + dresid_norm
    dresid_low = dresid.astype(jnp.bfloat16)
    grad_out = scatter_rel(attn, reorder(dresid_low), False)
    dattn = jnp.einsum("to,io->ti", dresid_low, full_out, preferred_element_type=jnp.float32)
    dattn = reorder(dattn.astype(jnp.bfloat16)).reshape(token_total, HEADS, HEAD_DIM)
    zeros_ext = jnp.zeros((token_total + 2 * WING, HEADS, HEAD_DIM), jnp.float32)

    def backward_block(carry, block_start):
        key_grad, value_grad = carry
        query_block, key_block, value_block, allowed = slices(block_start)
        probs = lax.dynamic_index_in_dim(stored, block_start // block_rows, 0, keepdims=False)
        dprobs = jnp.einsum("qhd,khd->hqk", dattn, value_block, preferred_element_type=jnp.float32)
        inner = jnp.sum(probs * dprobs, axis=-1, keepdims=True)
        dscores = (probs * (dprobs - inner)).astype(jnp.bfloat16)
        dquery = (
            jnp.einsum("hqk,khd->qhd", dscores, key_block, preferred_element_type=jnp.float32)
            * scaling
        )
        dkey = (
            jnp.einsum("hqk,qhd->khd", dscores, query_block, preferred_element_type=jnp.float32)
            * scaling
        )
        dvalue = jnp.einsum(
            "hqk,qhd->khd", probs.astype(jnp.bfloat16), dattn, preferred_element_type=jnp.float32
        )
        key_grad = key_grad + dkey
        value_grad = value_grad + dvalue
        return ((key_grad, value_grad), dquery)

    (key_grad, value_grad), dquery = lax.scan(backward_block, (zeros_ext, zeros_ext), starts)
    edge_grad = jnp.concatenate(
        [key_grad.reshape(-1, width), value_grad.reshape(-1, width)], axis=1
    )
    from_next = shifted(edge_grad[:WING].astype(jnp.bfloat16), ("seq", "wt"), -1).astype(
        jnp.float32
    )
    from_prev = shifted(
        edge_grad[token_total + WING :].astype(jnp.bfloat16), ("seq", "wt"), 1
    ).astype(jnp.float32)
    local_grad = edge_grad[WING : WING + token_total]
    local_grad = local_grad.at[:WING].add(from_prev).at[token_total - WING :].add(from_next)
    dquery_all = dquery.reshape(token_total, HEADS, HEAD_DIM)
    dkey_rot = local_grad[:, :width].reshape(token_total, HEADS, HEAD_DIM)
    dqkv = jnp.concatenate(
        [
            rotary_back(dquery_all, cosine, sine).reshape(token_total, width),
            rotary_back(dkey_rot, cosine, sine).reshape(token_total, width),
            local_grad[:, width:],
        ],
        axis=1,
    ).astype(jnp.bfloat16)
    grad_qkv = jnp.concatenate(
        [
            scatter_rel(act_one, dqkv[:, :cut], False),
            scatter_rel(act_one, dqkv[:, cut:], True),
        ],
        axis=1,
    )
    dact_one = jnp.einsum(
        "tf,df->td", dqkv[:, :cut], full_one, preferred_element_type=jnp.float32
    ) + jnp.einsum("tf,df->td", dqkv[:, cut:], full_two, preferred_element_type=jnp.float32)
    dinput_norm, grad_gain_attn = norm_one_back(dact_one)
    input_grad = reorder((dresid + dinput_norm).astype(jnp.bfloat16))
    gain_shares = scatter_gains(jnp.stack([grad_gain_attn, grad_gain_mlp]))
    return (
        block_output,
        input_grad,
        gain_shares[0],
        grad_qkv,
        grad_out,
        gain_shares[1],
        grad_in,
        grad_down,
    )


def solution(mesh):
    in_specs = (
        P(("seq", "wt"), None),
        P(("seq", "wt")),
        P(("seq", "wt")),
        P(("seq", "wt"), None),
        P(("seq", "wt"), None),
        P(("seq", "wt")),
        P(("seq", "wt"), None),
        P(("seq", "wt"), None),
        P(("seq", "wt"), None),
    )
    out_specs = (
        P(("seq", "wt"), None),
        P(("seq", "wt"), None),
        P(("seq", "wt")),
        P(("seq", "wt"), None),
        P(("seq", "wt"), None),
        P(("seq", "wt")),
        P(("seq", "wt"), None),
        P(("seq", "wt"), None),
    )
    return jax.shard_map(
        on_device, mesh=mesh, in_specs=in_specs, out_specs=out_specs, check_vma=False
    )
```

```python
import jax
import jax.numpy as jnp
from jax import lax
from jax.sharding import PartitionSpec as P

HEADS = 16
HEAD_DIM = 64
WING = 64


EPSILON = 1e-05


def padded_2(block, sides, width):
    for axis, dim in sides:
        count = lax.axis_size(axis)
        forward = [(i, i + 1) for i in range(count - 1)]
        backward = [(target, source) for source, target in forward]
        low = lax.ppermute(
            lax.slice_in_dim(block, block.shape[dim] - width, None, axis=dim), axis, forward
        )
        high = lax.ppermute(lax.slice_in_dim(block, 0, width, axis=dim), axis, backward)
        block = jnp.concatenate([low, block, high], axis=dim)
    return block


def shifted(block, axis, distance):
    devices = range(lax.axis_size(axis))
    route = [(i - distance, i) for i in devices if i - distance in devices]
    return lax.ppermute(block, axis, route)


def layer_norm(rows, gain):
    centered = rows - jnp.mean(rows, axis=-1, keepdims=True)
    spread = jnp.mean(centered * centered, axis=-1, keepdims=True)
    return centered * lax.rsqrt(spread + EPSILON) * gain


def rotate_half(vectors):
    middle = vectors.shape[-1] // 2
    return jnp.concatenate([-vectors[..., middle:], vectors[..., :middle]], axis=-1)


def angles(positions, head_width):
    middle = head_width // 2
    freqs = 10000.0 ** (-2.0 * jnp.arange(middle, dtype=jnp.float32) / head_width)
    phase = positions.astype(jnp.float32)[:, None] * freqs[None, :]
    phase = jnp.concatenate([phase, phase], axis=-1)[:, None, :]
    return (jnp.cos(phase), jnp.sin(phase))


def rotary(vectors, cosine, sine):
    return vectors * cosine + rotate_half(vectors) * sine


def rotary_back(grads, cosine, sine):
    return grads * cosine - rotate_half(grads * sine)


def gated(first, second):
    return jax.nn.gelu(first, approximate=False) * second


def device_count():
    return lax.axis_size(("seq", "wt"))


def swapped(block, mask):
    route = [(i, i ^ mask) for i in range(device_count())]
    return lax.ppermute(block, ("seq", "wt"), route)


def far_bits():
    near = lax.axis_size("wt")
    far = []
    bit = near
    while bit < device_count():
        far.append(bit)
        bit *= 2
    return near, far[0], far[:0:-1]


def block_masks():
    near, first, rest = far_bits()
    masks = [0]
    for bit in [first] + rest:
        masks = [mask | extra for mask in masks for extra in (0, bit)]
    return [mask | j for mask in masks for j in range(near)]


def gather_rel(block, flip):
    near, first, rest = far_bits()
    levels = len(rest)
    held = jnp.concatenate([block] + [swapped(block, j) for j in range(1, near)], axis=0)
    held = held.reshape((1,) * levels + held.shape)
    for bit in rest if flip else rest[::-1]:
        held = jnp.concatenate([held, swapped(held, bit)], axis=rest.index(bit))
    held = held.reshape(-1, block.shape[1])
    return held, swapped(held, first)


def scatter_begin(left, right, flip):
    near, first, rest = far_bits()
    width = left.shape[1]
    unit = width // (2 ** (len(rest) + 1))
    top = rest[0] if flip else rest[-1]
    place = len(rest) - 1 - rest.index(top)

    def product(core, second):
        base = core * width // 2
        picked = [k for k in range(2 ** len(rest)) if (k >> place) & 1 == second]
        part = jnp.concatenate(
            [left[:, base + k * unit : base + (k + 1) * unit] for k in picked], axis=1
        )
        return lax.dot_general(
            part, right, (((0,), (0,)), ((), ())), preferred_element_type=jnp.float32
        )

    got_far = swapped(product(1, 1).astype(jnp.bfloat16), first)
    got_near = swapped(product(1, 0).astype(jnp.bfloat16), first)
    far = (product(0, 1) + got_far.astype(jnp.float32)).astype(jnp.bfloat16)
    kept = product(0, 0) + got_near.astype(jnp.float32)
    return kept, swapped(far, top)


def scatter_end(begun, flip):
    near, first, rest = far_bits()
    kept, got = begun
    top = rest[0] if flip else rest[-1]
    total = kept + got.astype(jnp.float32)
    remaining = [bit for bit in rest if bit != top]
    rows = 2 * kept.shape[0] // (device_count() // 2)
    total = total.reshape((2,) * len(remaining) + (near, rows, kept.shape[1]))
    for axis, bit in enumerate(remaining):
        keep = lax.slice_in_dim(total, 0, 1, axis=axis)
        send = lax.slice_in_dim(total, 1, 2, axis=axis).astype(jnp.bfloat16)
        total = keep + swapped(send, bit).astype(jnp.float32)
    total = total.reshape(near, rows, kept.shape[1])
    result = total[0]
    for j in range(1, near):
        result = result + swapped(total[j].astype(jnp.bfloat16), j).astype(jnp.float32)
    return result


def scatter_gains(gains):
    near, first, rest = far_bits()
    total = gains.reshape(gains.shape[0], device_count(), -1).swapaxes(0, 1)
    bits = [first] + rest
    while near > 1:
        near //= 2
        bits.append(near)
    for bit in bits:
        half = total.shape[0] // 2
        total = total[:half] + swapped(total[half:], bit)
    return total[0]


def times(rows, halves):
    middle = rows.shape[1] // 2
    return jnp.dot(
        rows[:, :middle], halves[0], preferred_element_type=jnp.float32
    ) + jnp.dot(rows[:, middle:], halves[1], preferred_element_type=jnp.float32)


def times_transposed(rows, halves):
    return jnp.concatenate(
        [jnp.einsum("tf,df->td", rows, h, preferred_element_type=jnp.float32) for h in halves],
        axis=1,
    )


def block_mask(positions, block_start, block_rows, token_total, at_first, at_last):
    key_count = block_rows + 2 * WING
    query_index = block_start + jnp.arange(block_rows, dtype=jnp.int32)
    key_index = block_start - WING + jnp.arange(key_count, dtype=jnp.int32)
    padded = jnp.pad(positions, (WING, WING))
    offset = query_index[:, None] - key_index[None, :]
    inside = (key_index >= 0) & (key_index < token_total)
    same_doc = jnp.where(inside[None, :], positions[:, None] - padded[None, :] == offset, True)
    present = ((key_index >= 0) | jnp.logical_not(at_first)) & (
        (key_index < token_total) | jnp.logical_not(at_last)
    )
    return (jnp.abs(offset) <= WING) & same_doc & present[None, :]


def block_probs(query_block, key_block, allowed):
    scaling = HEAD_DIM ** (-0.5)
    scores = (
        jnp.einsum("qhd,khd->hqk", query_block, key_block, preferred_element_type=jnp.float32)
        * scaling
    )
    scores = jnp.where(allowed[None], scores, -1e30)
    largest = jnp.max(scores, axis=-1, keepdims=True)
    weights = jnp.exp(scores - largest)
    return weights / jnp.sum(weights, axis=-1, keepdims=True)


def on_device(
    block_input, positions, norm_gain_attn, w_qkv, w_out, norm_gain_mlp, w_in, w_down, cotangent
):
    token_total = block_input.shape[0]
    width = block_input.shape[1]
    scaling = HEAD_DIM ** (-0.5)
    device_index = lax.axis_index(("seq", "wt"))
    hidden_units = w_down.shape[1]
    cut = w_qkv.shape[1] // 2
    gains = jnp.stack([norm_gain_attn, norm_gain_mlp], axis=1)
    gains = jnp.pad(gains, ((0, 0), (0, 126)))
    full_one = gather_rel(jnp.concatenate([w_qkv[:, :cut], gains], axis=1), False)
    full_two = gather_rel(w_qkv[:, cut:], True)
    w_out, w_in, one, two = lax.optimization_barrier((w_out, w_in, full_one[0], full_two[0]))
    full_one, full_two = (one, full_one[1]), (two, full_two[1])
    full_out = gather_rel(w_out, False)
    full_first = gather_rel(w_in[:, :hidden_units], False)
    full_second = gather_rel(w_in[:, hidden_units:], True)
    w_down, one, two = lax.optimization_barrier((w_down, full_first[0], full_second[0]))
    full_first, full_second = (one, full_first[1]), (two, full_second[1])
    full_down = gather_rel(w_down, True)
    gathered = jnp.concatenate([half[:, cut : cut + 2] for half in full_one], axis=0)
    gain_attn, gain_mlp = gathered[:, 0], gathered[:, 1]
    full_one = [half[:, :cut] for half in full_one]
    rows = w_out.shape[0]
    masks = jnp.repeat(jnp.array(block_masks(), dtype=jnp.int32), rows) * rows
    columns = jnp.arange(width, dtype=jnp.int32)
    source = (masks + columns % rows) ^ (device_index * rows)
    swap = (columns[:, None] == source[None, :]).astype(jnp.bfloat16)

    def reorder(rows):
        return jnp.dot(rows, swap, preferred_element_type=jnp.float32).astype(jnp.bfloat16)

    def restore(rows):
        moved = jnp.einsum("tj,ij->ti", rows, swap, preferred_element_type=jnp.float32)
        return moved.astype(jnp.bfloat16)

    full_out = [reorder(half) for half in full_out]
    block_input = reorder(block_input)
    cotangent = reorder(cotangent)
    at_first = device_index == 0
    at_last = device_index == lax.axis_size(("seq", "wt")) - 1
    inputs = block_input.astype(jnp.float32)
    normed_one, norm_one_back = jax.vjp(layer_norm, inputs, gain_attn.astype(jnp.float32))
    act_one = normed_one.astype(jnp.bfloat16)
    qkv = jnp.concatenate(
        [
            times(act_one, full_one),
            times(act_one, full_two),
        ],
        axis=1,
    )
    cosine, sine = angles(positions, HEAD_DIM)
    query_rot = rotary(qkv[:, :width].reshape(token_total, HEADS, HEAD_DIM), cosine, sine).astype(
        jnp.bfloat16
    )
    key_rot = rotary(
        qkv[:, width : 2 * width].reshape(token_total, HEADS, HEAD_DIM), cosine, sine
    ).astype(jnp.bfloat16)
    value_low = qkv[:, 2 * width :].astype(jnp.bfloat16)
    paired = jnp.concatenate([key_rot.reshape(token_total, width), value_low], axis=1)
    edged = padded_2(paired, ((("seq", "wt"), 0),), WING)
    key_ext = edged[:, :width].reshape(-1, HEADS, HEAD_DIM)
    value_ext = edged[:, width:].reshape(-1, HEADS, HEAD_DIM)
    block_rows = min(512, token_total)
    starts = jnp.arange(token_total // block_rows, dtype=jnp.int32) * block_rows

    def slices(block_start):
        allowed = block_mask(positions, block_start, block_rows, token_total, at_first, at_last)
        return (query_rot, key_ext, value_ext, allowed)

    def forward_block(block_start):
        query_block, key_block, value_block, allowed = slices(block_start)
        probs = block_probs(query_block, key_block, allowed)
        mixed = jnp.einsum(
            "hqk,khd->qhd",
            probs.astype(jnp.bfloat16),
            value_block,
            preferred_element_type=jnp.float32,
        )
        return (mixed, probs)

    mixed, stored = lax.map(forward_block, starts)
    attn = reorder(mixed.reshape(token_total, width).astype(jnp.bfloat16))
    resid = inputs + times(attn, full_out)
    normed_two, norm_two_back = jax.vjp(layer_norm, resid, gain_mlp.astype(jnp.float32))
    act_two = normed_two.astype(jnp.bfloat16)
    first = times(act_two, full_first)
    second = times(act_two, full_second)
    gated_value, gated_back = jax.vjp(gated, first, second)
    hidden = gated_value.astype(jnp.bfloat16)
    output = resid + times_transposed(hidden, full_down)
    block_output = restore(output.astype(jnp.bfloat16))
    begun_down = scatter_begin(cotangent, hidden, True)
    dhidden = times(cotangent, full_down)
    dfirst, dsecond = gated_back(dhidden)
    dfirst = dfirst.astype(jnp.bfloat16)
    dsecond = dsecond.astype(jnp.bfloat16)
    begun_first = scatter_begin(act_two, dfirst, False)
    begun_second = scatter_begin(act_two, dsecond, True)
    dact_two = times_transposed(dfirst, full_first) + times_transposed(dsecond, full_second)
    dresid_norm, grad_gain_mlp = norm_two_back(dact_two)
    dresid = cotangent.astype(jnp.float32) + dresid_norm
    dresid_low = dresid.astype(jnp.bfloat16)
    dattn = restore(times_transposed(dresid_low, full_out).astype(jnp.bfloat16))
    dattn, begun_down = lax.optimization_barrier((dattn, begun_down))
    dattn = dattn.reshape(token_total, HEADS, HEAD_DIM)
    zeros_ext = jnp.zeros((token_total + 2 * WING, HEADS, HEAD_DIM), jnp.float32)

    def backward_block(carry, block_start):
        key_grad, value_grad = carry
        query_block, key_block, value_block, allowed = slices(block_start)
        probs = lax.dynamic_index_in_dim(stored, block_start // block_rows, 0, keepdims=False)
        dprobs = jnp.einsum("qhd,khd->hqk", dattn, value_block, preferred_element_type=jnp.float32)
        inner = jnp.sum(probs * dprobs, axis=-1, keepdims=True)
        dscores = (probs * (dprobs - inner)).astype(jnp.bfloat16)
        dquery = (
            jnp.einsum("hqk,khd->qhd", dscores, key_block, preferred_element_type=jnp.float32)
            * scaling
        )
        dkey = (
            jnp.einsum("hqk,qhd->khd", dscores, query_block, preferred_element_type=jnp.float32)
            * scaling
        )
        dvalue = jnp.einsum(
            "hqk,qhd->khd", probs.astype(jnp.bfloat16), dattn, preferred_element_type=jnp.float32
        )
        key_grad = key_grad + dkey
        value_grad = value_grad + dvalue
        return ((key_grad, value_grad), dquery)

    (key_grad, value_grad), dquery = lax.scan(backward_block, (zeros_ext, zeros_ext), starts)
    key_grad, value_grad, dquery, begun_first, begun_second = lax.optimization_barrier(
        (key_grad, value_grad, dquery, begun_first, begun_second)
    )
    grad_down = scatter_end(begun_down, True)
    grad_in = jnp.concatenate(
        [scatter_end(begun_first, False), scatter_end(begun_second, True)], axis=1
    )
    begun_out = scatter_begin(attn, restore(dresid_low), False)
    edge_grad = jnp.concatenate(
        [key_grad.reshape(-1, width), value_grad.reshape(-1, width)], axis=1
    )
    from_next = shifted(edge_grad[:WING].astype(jnp.bfloat16), ("seq", "wt"), -1).astype(
        jnp.float32
    )
    from_prev = shifted(
        edge_grad[token_total + WING :].astype(jnp.bfloat16), ("seq", "wt"), 1
    ).astype(jnp.float32)
    local_grad = edge_grad[WING : WING + token_total]
    local_grad = local_grad.at[:WING].add(from_prev).at[token_total - WING :].add(from_next)
    dquery_all = dquery.reshape(token_total, HEADS, HEAD_DIM)
    dkey_rot = local_grad[:, :width].reshape(token_total, HEADS, HEAD_DIM)
    dqkv = jnp.concatenate(
        [
            rotary_back(dquery_all, cosine, sine).reshape(token_total, width),
            rotary_back(dkey_rot, cosine, sine).reshape(token_total, width),
            local_grad[:, width:],
        ],
        axis=1,
    ).astype(jnp.bfloat16)
    begun_one = scatter_begin(act_one, dqkv[:, :cut], False)
    begun_two = scatter_begin(act_one, dqkv[:, cut:], True)
    grad_out = scatter_end(begun_out, False)
    grad_qkv = jnp.concatenate(
        [scatter_end(begun_one, False), scatter_end(begun_two, True)], axis=1
    )
    dact_one = times_transposed(dqkv[:, :cut], full_one) + times_transposed(
        dqkv[:, cut:], full_two
    )
    dinput_norm, grad_gain_attn = norm_one_back(dact_one)
    input_grad = restore((dresid + dinput_norm).astype(jnp.bfloat16))
    gain_shares = scatter_gains(jnp.stack([grad_gain_attn, grad_gain_mlp]))
    return (
        block_output,
        input_grad,
        gain_shares[0],
        grad_qkv,
        grad_out,
        gain_shares[1],
        grad_in,
        grad_down,
    )


def solution(mesh):
    in_specs = (
        P(("seq", "wt"), None),
        P(("seq", "wt")),
        P(("seq", "wt")),
        P(("seq", "wt"), None),
        P(("seq", "wt"), None),
        P(("seq", "wt")),
        P(("seq", "wt"), None),
        P(("seq", "wt"), None),
        P(("seq", "wt"), None),
    )
    out_specs = (
        P(("seq", "wt"), None),
        P(("seq", "wt"), None),
        P(("seq", "wt")),
        P(("seq", "wt"), None),
        P(("seq", "wt"), None),
        P(("seq", "wt")),
        P(("seq", "wt"), None),
        P(("seq", "wt"), None),
    )
    return jax.shard_map(
        on_device, mesh=mesh, in_specs=in_specs, out_specs=out_specs, check_vma=False
    )
```

```python
import jax
import jax.numpy as jnp
from jax import lax
from jax.sharding import PartitionSpec as P

HEADS = 16
HEAD_DIM = 64
WING = 64


EPSILON = 1e-05


def padded_2(block, sides, width):
    for axis, dim in sides:
        count = lax.axis_size(axis)
        forward = [(i, i + 1) for i in range(count - 1)]
        backward = [(target, source) for source, target in forward]
        low = lax.ppermute(
            lax.slice_in_dim(block, block.shape[dim] - width, None, axis=dim), axis, forward
        )
        high = lax.ppermute(lax.slice_in_dim(block, 0, width, axis=dim), axis, backward)
        block = jnp.concatenate([low, block, high], axis=dim)
    return block


def shifted(block, axis, distance):
    devices = range(lax.axis_size(axis))
    route = [(i - distance, i) for i in devices if i - distance in devices]
    return lax.ppermute(block, axis, route)


def layer_norm(rows, gain):
    centered = rows - jnp.mean(rows, axis=-1, keepdims=True)
    spread = jnp.mean(centered * centered, axis=-1, keepdims=True)
    return centered * lax.rsqrt(spread + EPSILON) * gain


def rotate_half(vectors):
    middle = vectors.shape[-1] // 2
    return jnp.concatenate([-vectors[..., middle:], vectors[..., :middle]], axis=-1)


def angles(positions, head_width):
    middle = head_width // 2
    freqs = 10000.0 ** (-2.0 * jnp.arange(middle, dtype=jnp.float32) / head_width)
    phase = positions.astype(jnp.float32)[:, None] * freqs[None, :]
    phase = jnp.concatenate([phase, phase], axis=-1)[:, None, :]
    return (jnp.cos(phase), jnp.sin(phase))


def rotary(vectors, cosine, sine):
    return vectors * cosine + rotate_half(vectors) * sine


def rotary_back(grads, cosine, sine):
    return grads * cosine - rotate_half(grads * sine)


def gated(first, second):
    return jax.nn.gelu(first, approximate=False) * second


def device_count():
    return lax.axis_size(("seq", "wt"))


def swapped(block, mask):
    route = [(i, i ^ mask) for i in range(device_count())]
    return lax.ppermute(block, ("seq", "wt"), route)


def far_bits():
    near = lax.axis_size("wt")
    far = []
    bit = near
    while bit < device_count():
        far.append(bit)
        bit *= 2
    return near, far[0], far[:0:-1]


def block_masks():
    near, first, rest = far_bits()
    masks = [0]
    for bit in [first] + rest:
        masks = [mask | extra for mask in masks for extra in (0, bit)]
    return [mask | j for mask in masks for j in range(near)]


def gather_rel(block, flip):
    near, first, rest = far_bits()
    levels = len(rest)
    held = jnp.concatenate([block] + [swapped(block, j) for j in range(1, near)], axis=0)
    held = held.reshape((1,) * levels + held.shape)
    for bit in rest if flip else rest[::-1]:
        held = jnp.concatenate([held, swapped(held, bit)], axis=rest.index(bit))
    held = held.reshape(-1, block.shape[1])
    return held, swapped(held, first)


def scatter_begin(left, right, flip):
    near, first, rest = far_bits()
    width = left.shape[1]
    unit = width // (2 ** (len(rest) + 1))
    top = rest[0] if flip else rest[-1]
    place = len(rest) - 1 - rest.index(top)

    def product(core, second):
        base = core * width // 2
        picked = [k for k in range(2 ** len(rest)) if (k >> place) & 1 == second]
        part = jnp.concatenate(
            [left[:, base + k * unit : base + (k + 1) * unit] for k in picked], axis=1
        )
        return lax.dot_general(
            part, right, (((0,), (0,)), ((), ())), preferred_element_type=jnp.float32
        )

    got_far = swapped(product(1, 1).astype(jnp.bfloat16), first)
    got_near = swapped(product(1, 0).astype(jnp.bfloat16), first)
    far = (product(0, 1) + got_far.astype(jnp.float32)).astype(jnp.bfloat16)
    kept = product(0, 0) + got_near.astype(jnp.float32)
    return kept, swapped(far, top)


def scatter_end(begun, flip):
    near, first, rest = far_bits()
    kept, got = begun
    top = rest[0] if flip else rest[-1]
    total = kept + got.astype(jnp.float32)
    remaining = [bit for bit in rest if bit != top]
    rows = 2 * kept.shape[0] // (device_count() // 2)
    total = total.reshape((2,) * len(remaining) + (near, rows, kept.shape[1]))
    for axis, bit in enumerate(remaining):
        keep = lax.slice_in_dim(total, 0, 1, axis=axis)
        send = lax.slice_in_dim(total, 1, 2, axis=axis).astype(jnp.bfloat16)
        total = keep + swapped(send, bit).astype(jnp.float32)
    total = total.reshape(near, rows, kept.shape[1])
    result = total[0]
    for j in range(1, near):
        result = result + swapped(total[j].astype(jnp.bfloat16), j).astype(jnp.float32)
    return result


def scatter_gains(gains):
    near, first, rest = far_bits()
    total = gains.reshape(gains.shape[0], device_count(), -1).swapaxes(0, 1)
    for bit in [first] + rest:
        half = total.shape[0] // 2
        total = total[:half] + swapped(total[half:], bit)
    return total[0] + sum(swapped(total[j], j) for j in range(1, near))


def times(rows, halves):
    middle = rows.shape[1] // 2
    return jnp.dot(
        rows[:, :middle], halves[0], preferred_element_type=jnp.float32
    ) + jnp.dot(rows[:, middle:], halves[1], preferred_element_type=jnp.float32)


def times_transposed(rows, halves):
    return jnp.concatenate(
        [jnp.einsum("tf,df->td", rows, h, preferred_element_type=jnp.float32) for h in halves],
        axis=1,
    )


def block_mask(positions, block_start, block_rows, token_total, at_first, at_last):
    key_count = block_rows + 2 * WING
    query_index = block_start + jnp.arange(block_rows, dtype=jnp.int32)
    key_index = block_start - WING + jnp.arange(key_count, dtype=jnp.int32)
    padded = jnp.pad(positions, (WING, WING))
    offset = query_index[:, None] - key_index[None, :]
    inside = (key_index >= 0) & (key_index < token_total)
    same_doc = jnp.where(inside[None, :], positions[:, None] - padded[None, :] == offset, True)
    present = ((key_index >= 0) | jnp.logical_not(at_first)) & (
        (key_index < token_total) | jnp.logical_not(at_last)
    )
    return (jnp.abs(offset) <= WING) & same_doc & present[None, :]


def block_probs(query_block, key_block, allowed):
    scaling = HEAD_DIM ** (-0.5)
    scores = (
        jnp.einsum("qhd,khd->hqk", query_block, key_block, preferred_element_type=jnp.float32)
        * scaling
    )
    scores = jnp.where(allowed[None], scores, -1e30)
    largest = jnp.max(scores, axis=-1, keepdims=True)
    weights = jnp.exp(scores - largest)
    return weights / jnp.sum(weights, axis=-1, keepdims=True)


def on_device(
    block_input, positions, norm_gain_attn, w_qkv, w_out, norm_gain_mlp, w_in, w_down, cotangent
):
    token_total = block_input.shape[0]
    width = block_input.shape[1]
    scaling = HEAD_DIM ** (-0.5)
    device_index = lax.axis_index(("seq", "wt"))
    hidden_units = w_down.shape[1]
    cut = w_qkv.shape[1] // 2
    gains = jnp.stack([norm_gain_attn, norm_gain_mlp], axis=1)
    gains = jnp.pad(gains, ((0, 0), (0, 126)))
    full_one = gather_rel(jnp.concatenate([w_qkv[:, :cut], gains], axis=1), False)
    full_two = gather_rel(w_qkv[:, cut:], True)
    w_out, w_in, full_one, full_two = lax.optimization_barrier((w_out, w_in, full_one, full_two))
    full_out = gather_rel(w_out, False)
    full_first = gather_rel(w_in[:, :hidden_units], False)
    full_second = gather_rel(w_in[:, hidden_units:], True)
    w_down, one, two = lax.optimization_barrier((w_down, full_first[0], full_second[0]))
    full_first, full_second = (one, full_first[1]), (two, full_second[1])
    full_down = gather_rel(w_down, True)
    gathered = jnp.concatenate([half[:, cut : cut + 2] for half in full_one], axis=0)
    gain_attn, gain_mlp = gathered[:, 0], gathered[:, 1]
    full_one = [half[:, :cut] for half in full_one]
    rows = w_out.shape[0]
    masks = jnp.repeat(jnp.array(block_masks(), dtype=jnp.int32), rows) * rows
    columns = jnp.arange(width, dtype=jnp.int32)
    source = (masks + columns % rows) ^ (device_index * rows)
    swap = (columns[:, None] == source[None, :]).astype(jnp.bfloat16)

    def reorder(rows):
        return jnp.dot(rows, swap, preferred_element_type=jnp.float32).astype(jnp.bfloat16)

    def restore(rows):
        moved = jnp.einsum("tj,ij->ti", rows, swap, preferred_element_type=jnp.float32)
        return moved.astype(jnp.bfloat16)

    full_out = [reorder(half) for half in full_out]
    block_input = reorder(block_input)
    cotangent = reorder(cotangent)
    at_first = device_index == 0
    at_last = device_index == lax.axis_size(("seq", "wt")) - 1
    inputs = block_input.astype(jnp.float32)
    normed_one, norm_one_back = jax.vjp(layer_norm, inputs, gain_attn.astype(jnp.float32))
    act_one = normed_one.astype(jnp.bfloat16)
    qkv = jnp.concatenate(
        [
            times(act_one, full_one),
            times(act_one, full_two),
        ],
        axis=1,
    )
    cosine, sine = angles(positions, HEAD_DIM)
    query_rot = rotary(qkv[:, :width].reshape(token_total, HEADS, HEAD_DIM), cosine, sine).astype(
        jnp.bfloat16
    )
    key_rot = rotary(
        qkv[:, width : 2 * width].reshape(token_total, HEADS, HEAD_DIM), cosine, sine
    ).astype(jnp.bfloat16)
    value_low = qkv[:, 2 * width :].astype(jnp.bfloat16)
    paired = jnp.concatenate([key_rot.reshape(token_total, width), value_low], axis=1)
    edged = padded_2(paired, ((("seq", "wt"), 0),), WING)
    key_ext = edged[:, :width].reshape(-1, HEADS, HEAD_DIM)
    value_ext = edged[:, width:].reshape(-1, HEADS, HEAD_DIM)
    block_rows = min(512, token_total)
    starts = jnp.arange(token_total // block_rows, dtype=jnp.int32) * block_rows

    def slices(block_start):
        allowed = block_mask(positions, block_start, block_rows, token_total, at_first, at_last)
        return (query_rot, key_ext, value_ext, allowed)

    def forward_block(block_start):
        query_block, key_block, value_block, allowed = slices(block_start)
        probs = block_probs(query_block, key_block, allowed)
        mixed = jnp.einsum(
            "hqk,khd->qhd",
            probs.astype(jnp.bfloat16),
            value_block,
            preferred_element_type=jnp.float32,
        )
        return (mixed, probs)

    mixed, stored = lax.map(forward_block, starts)
    attn = reorder(mixed.reshape(token_total, width).astype(jnp.bfloat16))
    resid = inputs + times(attn, full_out)
    normed_two, norm_two_back = jax.vjp(layer_norm, resid, gain_mlp.astype(jnp.float32))
    act_two = normed_two.astype(jnp.bfloat16)
    first = times(act_two, full_first)
    second = times(act_two, full_second)
    gated_value, gated_back = jax.vjp(gated, first, second)
    hidden = gated_value.astype(jnp.bfloat16)
    output = resid + times_transposed(hidden, full_down)
    block_output = restore(output.astype(jnp.bfloat16))
    begun_down = scatter_begin(cotangent, hidden, True)
    dhidden = times(cotangent, full_down)
    dfirst, dsecond = gated_back(dhidden)
    dfirst = dfirst.astype(jnp.bfloat16)
    dsecond = dsecond.astype(jnp.bfloat16)
    begun_first = scatter_begin(act_two, dfirst, False)
    begun_second = scatter_begin(act_two, dsecond, True)
    dact_two = times_transposed(dfirst, full_first) + times_transposed(dsecond, full_second)
    dresid_norm, grad_gain_mlp = norm_two_back(dact_two)
    dresid = cotangent.astype(jnp.float32) + dresid_norm
    dresid_low = dresid.astype(jnp.bfloat16)
    dattn = restore(times_transposed(dresid_low, full_out).astype(jnp.bfloat16))
    dattn, begun_down = lax.optimization_barrier((dattn, begun_down))
    dattn = dattn.reshape(token_total, HEADS, HEAD_DIM)
    zeros_ext = jnp.zeros((token_total + 2 * WING, HEADS, HEAD_DIM), jnp.float32)

    def backward_block(carry, block_start):
        key_grad, value_grad = carry
        query_block, key_block, value_block, allowed = slices(block_start)
        probs = lax.dynamic_index_in_dim(stored, block_start // block_rows, 0, keepdims=False)
        dprobs = jnp.einsum("qhd,khd->hqk", dattn, value_block, preferred_element_type=jnp.float32)
        inner = jnp.sum(probs * dprobs, axis=-1, keepdims=True)
        dscores = (probs * (dprobs - inner)).astype(jnp.bfloat16)
        dquery = (
            jnp.einsum("hqk,khd->qhd", dscores, key_block, preferred_element_type=jnp.float32)
            * scaling
        )
        dkey = (
            jnp.einsum("hqk,qhd->khd", dscores, query_block, preferred_element_type=jnp.float32)
            * scaling
        )
        dvalue = jnp.einsum(
            "hqk,qhd->khd", probs.astype(jnp.bfloat16), dattn, preferred_element_type=jnp.float32
        )
        key_grad = key_grad + dkey
        value_grad = value_grad + dvalue
        return ((key_grad, value_grad), dquery)

    (key_grad, value_grad), dquery = lax.scan(backward_block, (zeros_ext, zeros_ext), starts)
    key_grad, value_grad, dquery, begun_first, begun_second = lax.optimization_barrier(
        (key_grad, value_grad, dquery, begun_first, begun_second)
    )
    grad_down = scatter_end(begun_down, True)
    grad_in = jnp.concatenate(
        [scatter_end(begun_first, False), scatter_end(begun_second, True)], axis=1
    )
    begun_out = scatter_begin(attn, restore(dresid_low), False)
    edge_grad = jnp.concatenate(
        [key_grad.reshape(-1, width), value_grad.reshape(-1, width)], axis=1
    )
    from_next = shifted(edge_grad[:WING].astype(jnp.bfloat16), ("seq", "wt"), -1).astype(
        jnp.float32
    )
    from_prev = shifted(
        edge_grad[token_total + WING :].astype(jnp.bfloat16), ("seq", "wt"), 1
    ).astype(jnp.float32)
    local_grad = edge_grad[WING : WING + token_total]
    local_grad = local_grad.at[:WING].add(from_prev).at[token_total - WING :].add(from_next)
    dquery_all = dquery.reshape(token_total, HEADS, HEAD_DIM)
    dkey_rot = local_grad[:, :width].reshape(token_total, HEADS, HEAD_DIM)
    dqkv = jnp.concatenate(
        [
            rotary_back(dquery_all, cosine, sine).reshape(token_total, width),
            rotary_back(dkey_rot, cosine, sine).reshape(token_total, width),
            local_grad[:, width:],
        ],
        axis=1,
    ).astype(jnp.bfloat16)
    dqkv, grad_down, grad_in = lax.optimization_barrier((dqkv, grad_down, grad_in))
    begun_one = scatter_begin(act_one, dqkv[:, :cut], False)
    begun_two = scatter_begin(act_one, dqkv[:, cut:], True)
    grad_out = scatter_end(begun_out, False)
    dact_one = times_transposed(dqkv[:, :cut], full_one) + times_transposed(
        dqkv[:, cut:], full_two
    )
    dinput_norm, grad_gain_attn = norm_one_back(dact_one)
    gains, begun_one, begun_two = lax.optimization_barrier(
        (jnp.stack([grad_gain_attn, grad_gain_mlp]), begun_one, begun_two)
    )
    gain_shares = scatter_gains(gains)
    grad_qkv = jnp.concatenate(
        [scatter_end(begun_one, False), scatter_end(begun_two, True)], axis=1
    )
    input_grad = restore((dresid + dinput_norm).astype(jnp.bfloat16))
    return (
        block_output,
        input_grad,
        gain_shares[0],
        grad_qkv,
        grad_out,
        gain_shares[1],
        grad_in,
        grad_down,
    )


def solution(mesh):
    in_specs = (
        P(("seq", "wt"), None),
        P(("seq", "wt")),
        P(("seq", "wt")),
        P(("seq", "wt"), None),
        P(("seq", "wt"), None),
        P(("seq", "wt")),
        P(("seq", "wt"), None),
        P(("seq", "wt"), None),
        P(("seq", "wt"), None),
    )
    out_specs = (
        P(("seq", "wt"), None),
        P(("seq", "wt"), None),
        P(("seq", "wt")),
        P(("seq", "wt"), None),
        P(("seq", "wt"), None),
        P(("seq", "wt")),
        P(("seq", "wt"), None),
        P(("seq", "wt"), None),
    )
    return jax.shard_map(
        on_device, mesh=mesh, in_specs=in_specs, out_specs=out_specs, check_vma=False
    )
```
